128 devices in a mesh: user: 8 (over y_hi, z), item: 4 (over x), ctx: 4 (over y_lo, core).
Axes of the slice: x: 4, y: 4 (y_hi: 2, y_lo: 2; y = y_hi * 2 + y_lo), z: 4, core: 2. Of those that a mesh axis runs over, the one named last changes fastest.
Arguments:
- tile_values: bfloat16 [8, 4, 4, 16, 16, 128, 128], P('user', 'item', 'ctx'), may hold values from -127 to 127
- tile_weights: bfloat16 [8, 4, 4, 16, 16, 128, 128], P('user', 'item', 'ctx'), may hold values from 0 to 3
- tile_exponents: int32 [8, 4, 4, 16], P('user', 'item', 'ctx'), may hold values from -8 to -6
- tile_coords: int32 [8, 4, 4, 16, 3], P('user', 'item', 'ctx'), may hold values from 0 to 15, as said below
- tile_counts: int32 [8, 4, 4], P('user', 'item', 'ctx'), may hold values from 1 to 16, as said below
- user_factor: bfloat16 [8192, 256], P(('user', 'item', 'ctx')), may hold values from -2.5 to 2.5
- item_factor: bfloat16 [4096, 256], P(('item', 'user', 'ctx')), may hold values from -2.5 to 2.5
- context_factor: bfloat16 [1024, 256], P(('ctx', 'user', 'item')), may hold values from -2.5 to 2.5
Outputs:
- user_grad: float32 [8192, 256], P(('user', 'item', 'ctx'))
- item_grad: float32 [4096, 256], P(('item', 'user', 'ctx'))
- context_grad: float32 [1024, 256], P(('ctx', 'user', 'item'))
The draws below stay inside these ranges and needn't reach their ends.
Inputs may be any that keep to these rules, and one draw needn't show every extreme that they name: `tile_coords`: per grid cell: tile numbers below 8, 8 and 16 for the three columns, no two slots of a cell at the same tile. `tile_counts`: some grid cell has all 16 slots live.
All inputs are finite; a program needn't handle non-finite values.
Results may differ from the reference program's by a relative error of at most 0.0012.
Values may be sent and summed in bfloat16 or wider, within the bound.
A program may use at most 64 MiB of HBM per device.

```python
import jax
import jax.numpy as jnp
from jax import lax

RANK = 256
TILE_U = 128
TILE_I = 128
TILE_K = 16
UT = 8
IT = 8
CT = 16
TILES_DEV = 16
USERS = 8192
ITEMS = 4096
CTXS = 1024
N_USER = 8
N_ITEM = 4
N_CTX = 4


def draw_tile_values(key, part):
    key = jax.random.fold_in(key, 11)
    shape = (N_USER, N_ITEM, N_CTX, TILES_DEV, TILE_K, TILE_U, TILE_I)
    return jax.random.randint(key, shape, -127, 128).astype(jnp.float32).astype(jnp.bfloat16)


def draw_tile_weights(key, part):
    key = jax.random.fold_in(key, 12)
    shape = (N_USER, N_ITEM, N_CTX, TILES_DEV, TILE_K, TILE_U, TILE_I)
    return jax.random.randint(key, shape, 0, 4).astype(jnp.float32).astype(jnp.bfloat16)


def draw_tile_coords(key, part):
    key = jax.random.fold_in(key, 13)
    cells = N_USER * N_ITEM * N_CTX
    places_all = UT * IT * CT
    keys = jax.random.split(key, cells)
    places = jax.vmap(lambda one: jax.random.permutation(one, places_all)[:TILES_DEV])(keys).astype(jnp.int32)
    inner = (jax.random.permutation(jax.random.fold_in(key, 7), places_all - 2)[:TILES_DEV - 2] + 1).astype(jnp.int32)
    corner = jnp.array([places_all - 1, 0], jnp.int32)
    special = jnp.concatenate([corner, inner])
    chosen = jax.random.randint(jax.random.fold_in(key, 9), (), 0, cells)
    places = jnp.where((jnp.arange(cells, dtype=jnp.int32) == chosen)[:, None], special[None, :], places)
    user_tile = places // (IT * CT)
    item_tile = places // CT % IT
    ctx_tile = places % CT
    stacked = jnp.stack([user_tile, item_tile, ctx_tile], axis=-1)
    return stacked.reshape(N_USER, N_ITEM, N_CTX, TILES_DEV, 3)


def draw_tile_counts(key, part):
    key = jax.random.fold_in(key, 14)
    cells = N_USER * N_ITEM * N_CTX
    spread = jax.random.randint(key, (cells,), 0, TILES_DEV)
    counts = 1 + spread * spread // TILES_DEV
    fullest = jax.random.randint(jax.random.fold_in(key, 5), (), 0, cells)
    counts = jnp.where(jnp.arange(cells, dtype=jnp.int32) == fullest, TILES_DEV, counts)
    return counts.astype(jnp.int32).reshape(N_USER, N_ITEM, N_CTX)


def touch_ends(entries, key, least, high):
    dims = entries.shape
    index_at = [jax.random.randint(jax.random.fold_in(key, axis), (), 0, dims[axis]) for axis in range(len(dims))]
    entries = entries.at[tuple(index_at)].set(least)
    longest = dims.index(max(dims))
    index_at[longest] = (index_at[longest] + 1) % dims[longest]
    return entries.at[tuple(index_at)].set(high)


def block_scale(own_key, dims, pieces, least, largest):
    loudness = 1.0
    for dim, shards_of in pieces:
        heights = jax.random.uniform(jax.random.fold_in(jax.random.fold_in(own_key, 6), dim), (shards_of,), jnp.float32, least / len(pieces), largest / len(pieces))
        loudness = loudness * jnp.repeat(jnp.exp(heights), dims[dim] // shards_of).reshape((-1,) + (1,) * (len(dims) - 1 - dim))
    return loudness


def normal_values(stream_key, shape, scale, bound, cuts=(), kind=jnp.bfloat16):
    values = scale * jax.random.normal(stream_key, shape, jnp.float32)
    if cuts:
        values = values * block_scale(stream_key, shape, cuts, -0.22, 0.18)
    return jnp.clip(values, -bound, bound).astype(kind)


def setup_inputs(seed: int = 0) -> dict:
    key_list = jax.random.split(jax.random.key(seed), 9)
    return {
        "tile_values": draw_tile_values(jax.random.fold_in(key_list[8], 71), 0),
        "tile_weights": draw_tile_weights(jax.random.fold_in(key_list[8], 71), 0),
        "tile_exponents": touch_ends(jax.random.randint(key_list[2], (N_USER, N_ITEM, N_CTX, TILES_DEV), -8, -5), jax.random.fold_in(key_list[2], 1), -8, (-5) - 1).astype(jnp.int32),
        "tile_coords": draw_tile_coords(jax.random.fold_in(key_list[8], 71), 0),
        "tile_counts": draw_tile_counts(jax.random.fold_in(key_list[8], 71), 0),
        "user_factor": normal_values(key_list[5], (USERS, RANK), 0.4, 2.5, ((0, 128),)),
        "item_factor": normal_values(key_list[6], (ITEMS, RANK), 0.4, 2.5, ((0, 128),)),
        "context_factor": normal_values(key_list[7], (CTXS, RANK), 0.4, 2.5, ((0, 128),)),
    }


def tile_terms(a_rows, b_rows, g_rows, values, weights, exponent):
    scale = jnp.exp2(exponent.astype(jnp.float32))
    target = values.astype(jnp.float32) * scale
    depth, height, width = target.shape
    rank = a_rows.shape[1]
    product = (a_rows.astype(jnp.float32)[None, :, :] * g_rows.astype(jnp.float32)[:, None, :]).astype(jnp.bfloat16)
    flat_ag = product.reshape(depth * height, rank)
    model = jnp.dot(flat_ag, b_rows.T, preferred_element_type=jnp.float32)
    error = (weights.astype(jnp.float32).reshape(depth * height, width) * (model - target.reshape(depth * height, width))).astype(jnp.bfloat16)
    proj = jnp.dot(error, b_rows, preferred_element_type=jnp.float32).reshape(depth, height, rank)
    user_term = jnp.sum(proj * g_rows.astype(jnp.float32)[:, None, :], axis=0)
    ctx_term = jnp.sum(proj * a_rows.astype(jnp.float32)[None, :, :], axis=1)
    item_term = jnp.dot(error.T, flat_ag, preferred_element_type=jnp.float32)
    return user_term, item_term, ctx_term


def reference(tile_values, tile_weights, tile_exponents, tile_coords, tile_counts, user_factor, item_factor, context_factor):
    n_user, n_item, n_ctx = tile_counts.shape
    cells = n_user * n_item * n_ctx
    slots = tile_values.shape[3]
    user_block = UT * TILE_U
    item_block = IT * TILE_I
    ctx_block = CT * TILE_K
    values = tile_values.reshape((cells, slots) + tile_values.shape[4:])
    weights = tile_weights.reshape((cells, slots) + tile_weights.shape[4:])
    exponents = tile_exponents.reshape(cells, slots)
    coords = tile_coords.reshape(cells, slots, 3)
    counts = tile_counts.reshape(cells)
    ids = jnp.arange(cells, dtype=jnp.int32)

    def per_cell(carry, inputs):
        cell, cell_values, cell_weights, cell_exps, cell_coords, count = inputs
        user_base = (cell // (n_item * n_ctx)) * user_block
        item_base = ((cell // n_ctx) % n_item) * item_block
        ctx_base = (cell % n_ctx) * ctx_block

        def per_slot(inner, slot_inputs):
            grad_user, grad_item, grad_ctx = inner
            slot, slot_values, slot_weights, slot_exp, slot_coords = slot_inputs
            user_row = (user_base + slot_coords[0] * TILE_U).astype(jnp.int32)
            item_row = (item_base + slot_coords[1] * TILE_I).astype(jnp.int32)
            ctx_row = (ctx_base + slot_coords[2] * TILE_K).astype(jnp.int32)
            a_rows = lax.dynamic_slice_in_dim(user_factor, user_row, TILE_U, 0)
            b_rows = lax.dynamic_slice_in_dim(item_factor, item_row, TILE_I, 0)
            g_rows = lax.dynamic_slice_in_dim(context_factor, ctx_row, TILE_K, 0)
            user_term, item_term, ctx_term = tile_terms(a_rows, b_rows, g_rows, slot_values, slot_weights, slot_exp)
            live = (slot < count).astype(jnp.float32)
            zero = jnp.zeros((), jnp.int32)
            grad_user = lax.dynamic_update_slice(grad_user, lax.dynamic_slice_in_dim(grad_user, user_row, TILE_U, 0) + live * user_term, (user_row, zero))
            grad_item = lax.dynamic_update_slice(grad_item, lax.dynamic_slice_in_dim(grad_item, item_row, TILE_I, 0) + live * item_term, (item_row, zero))
            grad_ctx = lax.dynamic_update_slice(grad_ctx, lax.dynamic_slice_in_dim(grad_ctx, ctx_row, TILE_K, 0) + live * ctx_term, (ctx_row, zero))
            return (grad_user, grad_item, grad_ctx), None

        slot_ids = jnp.arange(slots, dtype=jnp.int32)
        carry, _ = lax.scan(per_slot, carry, (slot_ids, cell_values, cell_weights, cell_exps, cell_coords))
        return carry, None

    init = (jnp.zeros(user_factor.shape, jnp.float32), jnp.zeros(item_factor.shape, jnp.float32), jnp.zeros(context_factor.shape, jnp.float32))
    result, _ = lax.scan(per_cell, init, (ids, values, weights, exponents, coords, counts))
    return result[0], result[1], result[2]
```

```python
import functools

import jax
import jax.numpy as jnp
from jax import lax
from jax.experimental import pallas as pl
from jax.experimental.pallas import tpu as pltpu
from jax.sharding import PartitionSpec as P

MESH = pl.DeviceIdType.MESH
F32 = jnp.float32
BF16 = jnp.bfloat16
SLOTS, DEPTH, TU, TI, RANK = 16, 16, 128, 128, 256
UT, IT, CT = 8, 8, 16
NU, NI, NC = 8, 4, 4


def copy_to(src, dst, send, recv, device):
    return pltpu.make_async_remote_copy(
        src_ref=src,
        dst_ref=dst,
        send_sem=send,
        recv_sem=recv,
        device_id=device,
        device_id_type=MESH,
    )


def wait_bytes(ref, sem):
    pltpu.make_async_copy(ref, ref, sem).wait()


def kernel(
    values,
    weights,
    exps,
    coords,
    counts,
    uf,
    itf,
    cf,
    ug_out,
    ig_out,
    cg_out,
    vbuf,
    wbuf,
    ublk,
    iblk,
    cstage,
    cblk,
    gblk,
    ags,
    errs,
    iterms,
    uterms,
    cterms,
    prev,
    last,
    usum,
    isum,
    csum,
    umate,
    imate,
    urecv,
    irecv,
    crecv,
    load_sem,
    gsend,
    grecv,
    rsend,
    rrecv,
):
    u = lax.axis_index("user")
    i = lax.axis_index("item")
    c = lax.axis_index("ctx")
    ylo = c // 2
    core = c % 2
    mate = (u, i, ylo * 2 + 1 - core)
    uj = i * 2 + ylo
    ij = u * 2 + ylo
    cj = u * 4 + i

    def load(slot):
        return (
            pltpu.make_async_copy(
                values.at[0, 0, 0, slot], vbuf.at[slot], load_sem.at[0, slot]
            ),
            pltpu.make_async_copy(
                weights.at[0, 0, 0, slot], wbuf.at[slot], load_sem.at[1, slot]
            ),
        )

    def start_load(slot, carry):
        for copy in load(slot):
            copy.start()
        return carry

    lax.fori_loop(0, SLOTS, start_load, 0)

    def user_peer(d):
        j = (uj + d) % 8
        return (u, j // 2, (j % 2) * 2 + core)

    def item_peer(d):
        j = (ij + d) % 16
        return (j // 2, i, (j % 2) * 2 + core)

    def ctx_peer(d):
        j = (cj + d) % 32
        return (j // 4, j % 4, c)

    barrier = pltpu.get_barrier_semaphore()

    def greet(peer, n):
        def one(d, carry):
            pl.semaphore_signal(barrier, inc=1, device_id=peer(d), device_id_type=MESH)
            return carry

        lax.fori_loop(1, n, one, 0)

    greet(user_peer, 8)
    greet(item_peer, 16)
    greet(ctx_peer, 32)
    pl.semaphore_signal(barrier, inc=1, device_id=mate, device_id_type=MESH)

    ublk[core, uj] = uf[...]
    iblk[core, ij] = itf[...]
    own = cf[...].astype(F32)
    cstage[...] = jnp.concatenate([own[:, :128], own[:, 128:]], axis=0).astype(BF16)
    cblk[cj] = cstage[...]

    pl.semaphore_wait(barrier, 7 + 15 + 31 + 1)

    def gather_user(d, carry):
        copy_to(uf, ublk.at[core, uj], gsend.at[0], grecv.at[0], user_peer(d)).start()
        return carry

    def gather_item(d, carry):
        copy_to(itf, iblk.at[core, ij], gsend.at[1], grecv.at[1], item_peer(d)).start()
        return carry

    def gather_ctx(d, carry):
        copy_to(cstage, cblk.at[cj], gsend.at[2], grecv.at[2], ctx_peer(d)).start()
        return carry

    lax.fori_loop(1, 16, gather_item, 0)
    lax.fori_loop(1, 8, gather_user, 0)
    lax.fori_loop(1, 32, gather_ctx, 0)

    count = counts[0, 0, 0]
    tile = [[coords[0, 0, 0, s, m] for s in range(SLOTS)] for m in range(3)]
    for m in range(3):
        for s in range(SLOTS):
            entry = jnp.int32(0)
            for t in range(s):
                entry = jnp.where(tile[m][t] == tile[m][s], t + 1, entry)
            prev[m, s] = entry
        for n in range((UT, IT, CT)[m]):
            entry = jnp.int32(0)
            for s in range(SLOTS):
                hit = jnp.logical_and(tile[m][s] == n, s < count)
                entry = jnp.where(hit, s + 1, entry)
            last[m, n] = entry
    iterms[0] = jnp.zeros((TI, RANK), F32)
    uterms[0] = jnp.zeros((TU, RANK), F32)
    cterms[0] = jnp.zeros((DEPTH, RANK), F32)

    wait_bytes(iblk.at[0, pl.ds(0, 15)], grecv.at[1])
    item_forward = copy_to(
        iblk.at[core], iblk.at[core], gsend.at[3], grecv.at[3], mate
    )
    item_forward.start()
    wait_bytes(ublk.at[0, pl.ds(0, 7)], grecv.at[0])
    user_forward = copy_to(
        ublk.at[core], ublk.at[core], gsend.at[4], grecv.at[4], mate
    )
    user_forward.start()
    wait_bytes(cblk.at[pl.ds(0, 31)], grecv.at[2])

    def unpack_ctx(t, carry):
        rows = []
        for half in range(2):
            pair = cblk[2 * t + half].astype(F32)
            rows.append(jnp.concatenate([pair[:8], pair[8:]], axis=1))
        gblk[t] = jnp.concatenate(rows, axis=0)
        return carry

    lax.fori_loop(0, CT, unpack_ctx, 0)
    item_forward.wait()
    user_forward.wait()
    wait_bytes(ublk.at[0, pl.ds(0, 7)], gsend.at[0])
    wait_bytes(iblk.at[0, pl.ds(0, 15)], gsend.at[1])
    wait_bytes(cblk.at[pl.ds(0, 31)], gsend.at[2])

    def user_rows(slot):
        t = coords[0, 0, 0, slot, 0]
        return jnp.concatenate([ublk[0, t], ublk[1, t]], axis=0)

    def item_rows(slot):
        t = coords[0, 0, 0, slot, 1]
        return jnp.concatenate(
            [
                iblk[0, 2 * t],
                iblk[1, 2 * t],
                iblk[0, 2 * t + 1],
                iblk[1, 2 * t + 1],
            ],
            axis=0,
        )

    step = 2

    def phase_a(slot, carry):
        for copy in load(slot):
            copy.wait()
        a = user_rows(slot)
        b = item_rows(slot)
        g = gblk[coords[0, 0, 0, slot, 2]].astype(BF16)
        scale = lax.shift_left(jnp.int32(1), exps[0, 0, 0, slot] + 30).astype(F32) * (
            2.0**-30
        )
        for k in range(0, DEPTH, step):
            rows = pl.ds(k * TU, step * TU)
            ag = (a[None] * g[k : k + step][:, None, :]).reshape(step * TU, RANK)
            ags[rows] = ag
            model = lax.dot_general(
                ag, b, (((1,), (1,)), ((), ())), preferred_element_type=F32
            )
            w = wbuf[slot, k : k + step].reshape(step * TU, TI).astype(F32)
            v = vbuf[slot, k : k + step].reshape(step * TU, TI).astype(F32)
            errs[slot, rows] = (w * (model - v * scale)).astype(BF16)
        term = lax.dot_general(
            errs[slot], ags[...], (((0,), (0,)), ((), ())), preferred_element_type=F32
        )
        iterms[slot + 1] = term + iterms[prev[1, slot]]
        return carry

    def phase_b(slot, carry):
        a = user_rows(slot).astype(F32)
        b = item_rows(slot)
        g = gblk[coords[0, 0, 0, slot, 2]]
        total = uterms[prev[0, slot]]
        rows = []
        for k in range(DEPTH):
            proj = jnp.dot(
                errs[slot, pl.ds(k * TU, TU)], b, preferred_element_type=F32
            )
            total = total + proj * g[k : k + 1]
            rows.append(jnp.sum(proj * a, axis=0, keepdims=True))
        uterms[slot + 1] = total
        cterms[slot + 1] = jnp.concatenate(rows, axis=0) + cterms[prev[2, slot]]
        return carry

    lax.fori_loop(0, SLOTS, phase_a, 0)
    lax.fori_loop(0, SLOTS, phase_b, 0)

    for t in range(UT):
        rows = uterms[last[0, t]]
        usum[0, t] = rows[:64]
        usum[1, t] = rows[64:]
    user_mate = copy_to(
        usum.at[1 - core], umate, rsend.at[0], rrecv.at[0], mate
    )
    user_mate.start()
    for t in range(IT):
        rows = iterms[last[1, t]]
        isum[0, 2 * t] = rows[:32]
        isum[1, 2 * t] = rows[32:64]
        isum[0, 2 * t + 1] = rows[64:96]
        isum[1, 2 * t + 1] = rows[96:]
    item_mate = copy_to(
        isum.at[1 - core], imate, rsend.at[1], rrecv.at[1], mate
    )
    item_mate.start()
    for t in range(CT):
        rows = cterms[last[2, t]]
        csum[2 * t] = rows[:8]
        csum[2 * t + 1] = rows[8:]
    crecv[cj] = csum[cj]

    def scatter_ctx(d, carry):
        j = (cj + d) % 32
        copy_to(csum.at[j], crecv.at[cj], rsend.at[4], rrecv.at[4], ctx_peer(d)).start()
        return carry

    lax.fori_loop(1, 32, scatter_ctx, 0)

    user_mate.wait()
    for j in range(8):
        umate[j] += usum[core, j]
    urecv[uj] = umate[uj]

    def scatter_user(d, carry):
        j = (uj + d) % 8
        copy_to(umate.at[j], urecv.at[uj], rsend.at[2], rrecv.at[2], user_peer(d)).start()
        return carry

    lax.fori_loop(1, 8, scatter_user, 0)

    item_mate.wait()
    for j in range(16):
        imate[j] += isum[core, j]
    irecv[ij] = imate[ij]

    def scatter_item(d, carry):
        j = (ij + d) % 16
        copy_to(imate.at[j], irecv.at[ij], rsend.at[3], rrecv.at[3], item_peer(d)).start()
        return carry

    lax.fori_loop(1, 16, scatter_item, 0)

    wait_bytes(crecv.at[pl.ds(0, 31)], rrecv.at[4])
    cg_out[...] = jnp.sum(crecv[...], axis=0)
    wait_bytes(urecv.at[pl.ds(0, 7)], rrecv.at[2])
    ug_out[...] = jnp.sum(urecv[...], axis=0)
    wait_bytes(irecv.at[pl.ds(0, 15)], rrecv.at[3])
    ig_out[...] = jnp.sum(irecv[...], axis=0)
    wait_bytes(urecv.at[pl.ds(0, 7)], rsend.at[2])
    wait_bytes(irecv.at[pl.ds(0, 15)], rsend.at[3])
    wait_bytes(crecv.at[pl.ds(0, 31)], rsend.at[4])


def local(
    values,
    weights,
    exps,
    coords,
    counts,
    uf,
    itf,
    cf,
):
    hbm = pl.BlockSpec(memory_space=pltpu.HBM)
    smem = pl.BlockSpec(memory_space=pltpu.SMEM)
    vmem = pl.BlockSpec(memory_space=pltpu.VMEM)
    dma = pltpu.SemaphoreType.DMA
    return pl.pallas_call(
        kernel,
        in_specs=[hbm, hbm, smem, smem, smem, vmem, vmem, vmem],
        out_specs=[vmem, vmem, vmem],
        out_shape=[
            jax.ShapeDtypeStruct(uf.shape, F32),
            jax.ShapeDtypeStruct(itf.shape, F32),
            jax.ShapeDtypeStruct(cf.shape, F32),
        ],
        scratch_shapes=[
            pltpu.VMEM((SLOTS, DEPTH, TU, TI), BF16),
            pltpu.VMEM((SLOTS, DEPTH, TU, TI), BF16),
            pltpu.VMEM((2, 8, 64, RANK), BF16),
            pltpu.VMEM((2, 16, 32, RANK), BF16),
            pltpu.VMEM((16, 128), BF16),
            pltpu.VMEM((32, 16, 128), BF16),
            pltpu.VMEM((CT, DEPTH, RANK), F32),
            pltpu.VMEM((DEPTH * TU, RANK), BF16),
            pltpu.VMEM((SLOTS, DEPTH * TU, TI), BF16),
            pltpu.VMEM((SLOTS + 1, TI, RANK), F32),
            pltpu.VMEM((SLOTS + 1, TU, RANK), F32),
            pltpu.VMEM((SLOTS + 1, DEPTH, RANK), F32),
            pltpu.SMEM((3, SLOTS), jnp.int32),
            pltpu.SMEM((3, CT), jnp.int32),
            pltpu.VMEM((2, 8, 64, RANK), F32),
            pltpu.VMEM((2, 16, 32, RANK), F32),
            pltpu.VMEM((32, 8, RANK), F32),
            pltpu.VMEM((8, 64, RANK), F32),
            pltpu.VMEM((16, 32, RANK), F32),
            pltpu.VMEM((8, 64, RANK), F32),
            pltpu.VMEM((16, 32, RANK), F32),
            pltpu.VMEM((32, 8, RANK), F32),
            dma((2, SLOTS)),
            dma((5,)),
            dma((5,)),
            dma((5,)),
            dma((5,)),
        ],
        compiler_params=pltpu.CompilerParams(
            collective_id=0,
            has_side_effects=True,
            vmem_limit_bytes=56 * 2**20,
        ),
        name="cp_gradient",
    )(values, weights, exps, coords, counts, uf, itf, cf)


def solution(mesh):
    placed = (
        P("user", "item", "ctx", None, None, None, None),
        P("user", "item", "ctx", None, None, None, None),
        P("user", "item", "ctx", None),
        P("user", "item", "ctx", None, None),
        P("user", "item", "ctx"),
        P(("user", "item", "ctx"), None),
        P(("item", "user", "ctx"), None),
        P(("ctx", "user", "item"), None),
    )
    return jax.shard_map(
        local,
        mesh=mesh,
        in_specs=placed,
        out_specs=(
            P(("user", "item", "ctx"), None),
            P(("item", "user", "ctx"), None),
            P(("ctx", "user", "item"), None),
        ),
        check_vma=False,
    )
```

```python
import functools

import jax
import jax.numpy as jnp
from jax import lax
from jax.experimental import pallas as pl
from jax.experimental.pallas import tpu as pltpu
from jax.sharding import PartitionSpec as P

MESH = pl.DeviceIdType.MESH
F32 = jnp.float32
BF16 = jnp.bfloat16
SLOTS, DEPTH, TU, TI, RANK = 16, 16, 128, 128, 256
UT, IT, CT = 8, 8, 16
NU, NI, NC = 8, 4, 4


def copy_to(src, dst, send, recv, device):
    return pltpu.make_async_remote_copy(
        src_ref=src,
        dst_ref=dst,
        send_sem=send,
        recv_sem=recv,
        device_id=device,
        device_id_type=MESH,
    )


def wait_bytes(ref, sem):
    pltpu.make_async_copy(ref, ref, sem).wait()


def kernel(
    values,
    weights,
    exps,
    coords,
    counts,
    uf,
    itf,
    cf,
    ug_out,
    ig_out,
    cg_out,
    vbuf,
    wbuf,
    ublk,
    iblk,
    cstage,
    cblk,
    gblk,
    errs,
    iterms,
    uterms,
    cterms,
    prev,
    last,
    usum,
    isum,
    csum,
    umate,
    imate,
    urecv,
    irecv,
    crecv,
    load_sem,
    gsend,
    grecv,
    rsend,
    rrecv,
):
    u = lax.axis_index("user")
    i = lax.axis_index("item")
    c = lax.axis_index("ctx")
    ylo = c // 2
    core = c % 2
    mate = (u, i, ylo * 2 + 1 - core)
    uj = i * 2 + ylo
    ij = u * 2 + ylo
    cj = u * 4 + i

    def load(slot):
        return (
            pltpu.make_async_copy(
                values.at[0, 0, 0, slot], vbuf.at[slot], load_sem.at[0, slot]
            ),
            pltpu.make_async_copy(
                weights.at[0, 0, 0, slot], wbuf.at[slot], load_sem.at[1, slot]
            ),
        )

    def start_load(slot, carry):
        for copy in load(slot):
            copy.start()
        return carry

    lax.fori_loop(0, SLOTS, start_load, 0)

    def user_peer(d):
        j = (uj + d) % 8
        return (u, j // 2, (j % 2) * 2 + core)

    def item_peer(d):
        j = (ij + d) % 16
        return (j // 2, i, (j % 2) * 2 + core)

    def ctx_peer(d):
        j = (cj + d) % 32
        return (j // 4, j % 4, c)

    barrier = pltpu.get_barrier_semaphore()

    def greet(peer, n):
        def one(d, carry):
            pl.semaphore_signal(barrier, inc=1, device_id=peer(d), device_id_type=MESH)
            return carry

        lax.fori_loop(1, n, one, 0)

    greet(user_peer, 8)
    greet(item_peer, 16)
    greet(ctx_peer, 32)
    pl.semaphore_signal(barrier, inc=1, device_id=mate, device_id_type=MESH)

    ublk[core, uj] = uf[...]
    iblk[core, ij] = itf[...]
    own = cf[...].astype(F32)
    cstage[...] = jnp.concatenate([own[:, :128], own[:, 128:]], axis=0).astype(BF16)
    cblk[cj] = cstage[...]

    pl.semaphore_wait(barrier, 7 + 15 + 31 + 1)

    def gather_user(d, carry):
        copy_to(uf, ublk.at[core, uj], gsend.at[0], grecv.at[0], user_peer(d)).start()
        return carry

    def gather_item(d, carry):
        copy_to(itf, iblk.at[core, ij], gsend.at[1], grecv.at[1], item_peer(d)).start()
        return carry

    def gather_ctx(d, carry):
        copy_to(cstage, cblk.at[cj], gsend.at[2], grecv.at[2], ctx_peer(d)).start()
        return carry

    lax.fori_loop(1, 16, gather_item, 0)
    lax.fori_loop(1, 8, gather_user, 0)
    lax.fori_loop(1, 32, gather_ctx, 0)

    count = counts[0, 0, 0]
    tile = [[coords[0, 0, m, 0, s] for s in range(SLOTS)] for m in range(3)]
    for m in range(3):
        for s in range(SLOTS):
            entry = jnp.int32(0)
            for t in range(s):
                entry = jnp.where(tile[m][t] == tile[m][s], t + 1, entry)
            prev[m, s] = entry
        for n in range((UT, IT, CT)[m]):
            entry = jnp.int32(0)
            for s in range(SLOTS):
                hit = jnp.logical_and(tile[m][s] == n, s < count)
                entry = jnp.where(hit, s + 1, entry)
            last[m, n] = entry
    iterms[0] = jnp.zeros((TI, RANK), F32)
    for order in range(2):
        uterms[order, 0] = jnp.zeros((64, RANK), F32)
        cterms[order, 0] = jnp.zeros((DEPTH, RANK), F32)

    wait_bytes(iblk.at[0, pl.ds(0, 15)], grecv.at[1])
    item_forward = copy_to(
        iblk.at[core], iblk.at[core], gsend.at[3], grecv.at[3], mate
    )
    item_forward.start()
    wait_bytes(ublk.at[0, pl.ds(0, 7)], grecv.at[0])
    user_forward = copy_to(
        ublk.at[core], ublk.at[core], gsend.at[4], grecv.at[4], mate
    )
    user_forward.start()
    wait_bytes(cblk.at[pl.ds(0, 31)], grecv.at[2])

    def unpack_ctx(t, carry):
        rows = []
        for half in range(2):
            pair = cblk[2 * t + half].astype(F32)
            rows.append(jnp.concatenate([pair[:8], pair[8:]], axis=1))
        gblk[t] = jnp.concatenate(rows, axis=0)
        return carry

    lax.fori_loop(0, CT, unpack_ctx, 0)
    item_forward.wait()
    user_forward.wait()
    wait_bytes(ublk.at[0, pl.ds(0, 7)], gsend.at[0])
    wait_bytes(iblk.at[0, pl.ds(0, 15)], gsend.at[1])
    wait_bytes(cblk.at[pl.ds(0, 31)], gsend.at[2])

    def item_rows(slot):
        t = coords[0, 0, 1, 0, slot]
        return jnp.concatenate(
            [
                iblk[0, 2 * t],
                iblk[1, 2 * t],
                iblk[0, 2 * t + 1],
                iblk[1, 2 * t + 1],
            ],
            axis=0,
        )

    step = 4

    def end_load(slot, carry):
        for copy in load(slot):
            copy.wait()
        return carry

    lax.fori_loop(0, SLOTS, end_load, 0)

    def phase_a(slot, carry):
        t = coords[0, 0, 0, 0, slot]
        a = jnp.concatenate([ublk[0, t], ublk[1, t]], axis=0)
        b = item_rows(slot)
        g = gblk[coords[0, 0, 2, 0, slot]].astype(BF16)
        scale = lax.shift_left(jnp.int32(1), exps[0, 0, 0, slot] + 30).astype(F32) * (
            2.0**-30
        )
        term = jnp.zeros((TI, RANK), F32)
        for k in range(0, DEPTH, step):
            ag = (a[None] * g[k : k + step][:, None, :]).reshape(step * TU, RANK)
            model = lax.dot_general(
                ag, b, (((1,), (1,)), ((), ())), preferred_element_type=F32
            )
            w = wbuf[slot, k : k + step].reshape(step * TU, TI).astype(F32)
            v = vbuf[slot, k : k + step].reshape(step * TU, TI).astype(F32)
            err = (w * (model - v * scale)).astype(BF16)
            for n in range(step):
                errs[slot, 0, k + n] = err[n * TU : n * TU + 64]
                errs[slot, 1, k + n] = err[n * TU + 64 : n * TU + TU]
            term = term + lax.dot_general(
                err, ag, (((0,), (0,)), ((), ())), preferred_element_type=F32
            )
        iterms[slot + 1] = term + iterms[prev[1, slot]]
        return carry

    def phase_b(order, slot, carry):
        half = core if order else 1 - core
        a = ublk[half, coords[0, 0, 0, 0, slot]].astype(F32)
        b = item_rows(slot)
        g = gblk[coords[0, 0, 2, 0, slot]]
        total = jnp.zeros((64, RANK), F32)
        rows = []
        for k in range(DEPTH):
            proj = jnp.dot(errs[slot, half, k], b, preferred_element_type=F32)
            total = total + proj * g[k : k + 1]
            rows.append(jnp.sum(proj * a, axis=0, keepdims=True))
        uterms[order, slot + 1] = total + uterms[order, prev[0, slot]]
        cterms[order, slot + 1] = (
            jnp.concatenate(rows, axis=0) + cterms[order, prev[2, slot]]
        )
        return carry

    lax.fori_loop(0, SLOTS, phase_a, 0, unroll=4)

    for t in range(IT):
        rows = iterms[last[1, t]]
        isum[0, 2 * t] = rows[:32]
        isum[1, 2 * t] = rows[32:64]
        isum[0, 2 * t + 1] = rows[64:96]
        isum[1, 2 * t + 1] = rows[96:]
    item_mate = copy_to(isum.at[1 - core], imate, rsend.at[1], rrecv.at[1], mate)
    item_mate.start()

    lax.fori_loop(0, SLOTS, functools.partial(phase_b, 0), 0, unroll=4)

    for t in range(UT):
        usum[t] = uterms[0, last[0, t]]
    user_mate = copy_to(usum, umate, rsend.at[0], rrecv.at[0], mate)
    user_mate.start()

    item_mate.wait()
    for j in range(16):
        imate[j] += isum[core, j]
    irecv[ij] = imate[ij]

    def scatter_item(d, carry):
        j = (ij + d) % 16
        copy_to(imate.at[j], irecv.at[ij], rsend.at[3], rrecv.at[3], item_peer(d)).start()
        return carry

    lax.fori_loop(1, 16, scatter_item, 0)

    lax.fori_loop(0, SLOTS, functools.partial(phase_b, 1), 0, unroll=4)

    user_mate.wait()
    for t in range(UT):
        umate[t] += uterms[1, last[0, t]]
    urecv[uj] = umate[uj]

    def scatter_user(d, carry):
        j = (uj + d) % 8
        copy_to(umate.at[j], urecv.at[uj], rsend.at[2], rrecv.at[2], user_peer(d)).start()
        return carry

    lax.fori_loop(1, 8, scatter_user, 0)

    for t in range(CT):
        rows = cterms[0, last[2, t]] + cterms[1, last[2, t]]
        csum[2 * t] = rows[:8]
        csum[2 * t + 1] = rows[8:]
    crecv[cj] = csum[cj]

    def scatter_ctx(d, carry):
        j = (cj + d) % 32
        copy_to(csum.at[j], crecv.at[cj], rsend.at[4], rrecv.at[4], ctx_peer(d)).start()
        return carry

    lax.fori_loop(1, 32, scatter_ctx, 0)

    wait_bytes(irecv.at[pl.ds(0, 15)], rrecv.at[3])
    ig_out[...] = jnp.sum(irecv[...], axis=0)
    wait_bytes(urecv.at[pl.ds(0, 7)], rrecv.at[2])
    ug_out[...] = jnp.sum(urecv[...], axis=0)
    wait_bytes(crecv.at[pl.ds(0, 31)], rrecv.at[4])
    cg_out[...] = jnp.sum(crecv[...], axis=0)
    wait_bytes(urecv.at[pl.ds(0, 7)], rsend.at[2])
    wait_bytes(irecv.at[pl.ds(0, 15)], rsend.at[3])
    wait_bytes(crecv.at[pl.ds(0, 31)], rsend.at[4])


def copy_out(ug, ig, cg, ug_out, ig_out, cg_out):
    ug_out[...] = ug[...]
    ig_out[...] = ig[...]
    cg_out[...] = cg[...]


def local(
    values,
    weights,
    exps,
    coords,
    counts,
    uf,
    itf,
    cf,
):
    hbm = pl.BlockSpec(memory_space=pltpu.HBM)
    smem = pl.BlockSpec(memory_space=pltpu.SMEM)
    vmem = pl.BlockSpec(memory_space=pltpu.VMEM)
    dma = pltpu.SemaphoreType.DMA
    grads = pl.pallas_call(
        kernel,
        in_specs=[hbm, hbm, smem, smem, smem, vmem, vmem, vmem],
        out_specs=[vmem, vmem, vmem],
        out_shape=[
            jax.ShapeDtypeStruct(uf.shape, F32),
            jax.ShapeDtypeStruct(itf.shape, F32),
            jax.ShapeDtypeStruct(cf.shape, F32),
        ],
        scratch_shapes=[
            pltpu.VMEM((SLOTS, DEPTH, TU, TI), BF16),
            pltpu.VMEM((SLOTS, DEPTH, TU, TI), BF16),
            pltpu.VMEM((2, 8, 64, RANK), BF16),
            pltpu.VMEM((2, 16, 32, RANK), BF16),
            pltpu.VMEM((16, 128), BF16),
            pltpu.VMEM((32, 16, 128), BF16),
            pltpu.VMEM((CT, DEPTH, RANK), F32),
            pltpu.VMEM((SLOTS, 2, DEPTH, 64, TI), BF16),
            pltpu.VMEM((SLOTS + 1, TI, RANK), F32),
            pltpu.VMEM((2, SLOTS + 1, 64, RANK), F32),
            pltpu.VMEM((2, SLOTS + 1, DEPTH, RANK), F32),
            pltpu.SMEM((3, SLOTS), jnp.int32),
            pltpu.SMEM((3, CT), jnp.int32),
            pltpu.VMEM((8, 64, RANK), F32),
            pltpu.VMEM((2, 16, 32, RANK), F32),
            pltpu.VMEM((32, 8, RANK), F32),
            pltpu.VMEM((8, 64, RANK), F32),
            pltpu.VMEM((16, 32, RANK), F32),
            pltpu.VMEM((8, 64, RANK), F32),
            pltpu.VMEM((16, 32, RANK), F32),
            pltpu.VMEM((32, 8, RANK), F32),
            dma((2, SLOTS)),
            dma((5,)),
            dma((5,)),
            dma((5,)),
            dma((5,)),
        ],
        compiler_params=pltpu.CompilerParams(
            collective_id=0,
            has_side_effects=True,
            vmem_limit_bytes=56 * 2**20,
        ),
        name="cp_gradient",
    )(values, weights, exps, jnp.transpose(coords, (0, 1, 4, 2, 3)), counts, uf, itf, cf)
    return pl.pallas_call(
        copy_out,
        in_specs=[vmem] * 3,
        out_specs=[vmem] * 3,
        out_shape=[jax.ShapeDtypeStruct(g.shape, F32) for g in grads],
        name="copy_out",
    )(*grads)


def solution(mesh):
    placed = (
        P("user", "item", "ctx", None, None, None, None),
        P("user", "item", "ctx", None, None, None, None),
        P("user", "item", "ctx", None),
        P("user", "item", "ctx", None, None),
        P("user", "item", "ctx"),
        P(("user", "item", "ctx"), None),
        P(("item", "user", "ctx"), None),
        P(("ctx", "user", "item"), None),
    )
    return jax.shard_map(
        local,
        mesh=mesh,
        in_specs=placed,
        out_specs=(
            P(("user", "item", "ctx"), None),
            P(("item", "user", "ctx"), None),
            P(("ctx", "user", "item"), None),
        ),
        check_vma=False,
    )
```

```python
import functools

import jax
import jax.numpy as jnp
from jax import lax
from jax.experimental import pallas as pl
from jax.experimental.pallas import tpu as pltpu
from jax.sharding import PartitionSpec as P

MESH = pl.DeviceIdType.MESH
F32 = jnp.float32
BF16 = jnp.bfloat16
SLOTS, DEPTH, TU, TI, RANK = 16, 16, 128, 128, 256
UT, IT, CT = 8, 8, 16
NU, NI, NC = 8, 4, 4


def copy_to(src, dst, send, recv, device):
    return pltpu.make_async_remote_copy(
        src_ref=src,
        dst_ref=dst,
        send_sem=send,
        recv_sem=recv,
        device_id=device,
        device_id_type=MESH,
    )


def wait_bytes(ref, sem):
    pltpu.make_async_copy(ref, ref, sem).wait()


def pack(rows):
    left, right = rows[:, :128], rows[:, 128:]
    peak = jnp.max(jnp.maximum(jnp.abs(left), jnp.abs(right)), axis=0, keepdims=True)
    power = jnp.floor(jnp.log2(jnp.maximum(peak, 2.0**-90))) + 1.0
    scale = jnp.exp2(-power) * 32000.0
    high = jnp.round(left * scale).astype(jnp.int32)
    low = jnp.round(right * scale).astype(jnp.int32)
    codes = lax.shift_left(high, 16) | (low & 0xFFFF)
    return codes, power.astype(jnp.int32)


def unpack(ref, j, n):
    codes = ref[j, :n]
    step = jnp.exp2(ref[j, n : n + 1].astype(F32)) * (1.0 / 32000.0)
    high = lax.shift_right_arithmetic(codes, 16).astype(F32)
    low = lax.shift_right_arithmetic(lax.shift_left(codes, 16), 16).astype(F32)
    return jnp.concatenate([high * step, low * step], axis=1)


def kernel(
    values,
    weights,
    exps,
    coords,
    counts,
    uf,
    itf,
    cf,
    ug_out,
    ig_out,
    cg_out,
    vbuf,
    wbuf,
    ublk,
    iblk,
    cstage,
    cblk,
    gblk,
    errs,
    iterms,
    uterms,
    cterms,
    prev,
    last,
    usum,
    isum,
    csum,
    umate,
    imate,
    usend,
    isend,
    csend,
    urecv,
    irecv,
    crecv,
    load_sem,
    gsend,
    grecv,
    rsend,
    rrecv,
):
    u = lax.axis_index("user")
    i = lax.axis_index("item")
    c = lax.axis_index("ctx")
    ylo = c // 2
    core = c % 2
    mate = (u, i, ylo * 2 + 1 - core)
    uj = i * 2 + ylo
    ij = u * 2 + ylo
    cj = u * 4 + i

    def load(slot):
        return (
            pltpu.make_async_copy(
                values.at[0, 0, 0, slot], vbuf.at[slot], load_sem.at[0, slot]
            ),
            pltpu.make_async_copy(
                weights.at[0, 0, 0, slot], wbuf.at[slot], load_sem.at[1, slot]
            ),
        )

    def start_load(slot, carry):
        for copy in load(slot):
            copy.start()
        return carry

    lax.fori_loop(0, SLOTS, start_load, 0)

    def user_peer(d):
        j = (uj + d) % 8
        return (u, j // 2, (j % 2) * 2 + core)

    def item_peer(d):
        j = (ij + d) % 16
        return (j // 2, i, (j % 2) * 2 + core)

    def ctx_peer(d):
        j = (cj + d) % 32
        return (j // 4, j % 4, c)

    barrier = pltpu.get_barrier_semaphore()

    def greet(peer, n):
        def one(d, carry):
            pl.semaphore_signal(barrier, inc=1, device_id=peer(d), device_id_type=MESH)
            return carry

        lax.fori_loop(1, n, one, 0)

    greet(user_peer, 8)
    greet(item_peer, 16)
    greet(ctx_peer, 32)
    pl.semaphore_signal(barrier, inc=1, device_id=mate, device_id_type=MESH)

    ublk[core, uj] = uf[...]
    iblk[core, ij] = itf[...]
    own = cf[...].astype(F32)
    cstage[...] = jnp.concatenate([own[:, :128], own[:, 128:]], axis=0).astype(BF16)
    cblk[cj] = cstage[...]

    pl.semaphore_wait(barrier, 7 + 15 + 31 + 1)

    def gather_user(d, carry):
        copy_to(uf, ublk.at[core, uj], gsend.at[0], grecv.at[0], user_peer(d)).start()
        return carry

    def gather_item(d, carry):
        copy_to(itf, iblk.at[core, ij], gsend.at[1], grecv.at[1], item_peer(d)).start()
        return carry

    def gather_ctx(d, carry):
        copy_to(cstage, cblk.at[cj], gsend.at[2], grecv.at[2], ctx_peer(d)).start()
        return carry

    lax.fori_loop(1, 16, gather_item, 0)
    lax.fori_loop(1, 8, gather_user, 0)
    lax.fori_loop(1, 32, gather_ctx, 0)

    count = counts[0, 0, 0]
    tile = [[coords[0, 0, m, 0, s] for s in range(SLOTS)] for m in range(3)]
    for m in range(3):
        for s in range(SLOTS):
            entry = jnp.int32(0)
            for t in range(s):
                entry = jnp.where(tile[m][t] == tile[m][s], t + 1, entry)
            prev[m, s] = entry
        for n in range((UT, IT, CT)[m]):
            entry = jnp.int32(0)
            for s in range(SLOTS):
                hit = jnp.logical_and(tile[m][s] == n, s < count)
                entry = jnp.where(hit, s + 1, entry)
            last[m, n] = entry
    iterms[0] = jnp.zeros((TI, RANK), F32)
    for order in range(2):
        uterms[order, 0] = jnp.zeros((64, RANK), F32)
        cterms[order, 0] = jnp.zeros((DEPTH, RANK), F32)

    wait_bytes(iblk.at[0, pl.ds(0, 15)], grecv.at[1])
    item_forward = copy_to(
        iblk.at[core], iblk.at[core], gsend.at[3], grecv.at[3], mate
    )
    item_forward.start()
    wait_bytes(ublk.at[0, pl.ds(0, 7)], grecv.at[0])
    user_forward = copy_to(
        ublk.at[core], ublk.at[core], gsend.at[4], grecv.at[4], mate
    )
    user_forward.start()
    wait_bytes(cblk.at[pl.ds(0, 31)], grecv.at[2])

    def unpack_ctx(t, carry):
        rows = []
        for half in range(2):
            pair = cblk[2 * t + half].astype(F32)
            rows.append(jnp.concatenate([pair[:8], pair[8:]], axis=1))
        gblk[t] = jnp.concatenate(rows, axis=0)
        return carry

    lax.fori_loop(0, CT, unpack_ctx, 0)
    item_forward.wait()
    user_forward.wait()
    wait_bytes(ublk.at[0, pl.ds(0, 7)], gsend.at[0])
    wait_bytes(iblk.at[0, pl.ds(0, 15)], gsend.at[1])
    wait_bytes(cblk.at[pl.ds(0, 31)], gsend.at[2])

    def item_rows(slot):
        t = coords[0, 0, 1, 0, slot]
        return jnp.concatenate(
            [
                iblk[0, 2 * t],
                iblk[1, 2 * t],
                iblk[0, 2 * t + 1],
                iblk[1, 2 * t + 1],
            ],
            axis=0,
        )

    step = 4

    def end_load(slot, carry):
        for copy in load(slot):
            copy.wait()
        return carry

    lax.fori_loop(0, SLOTS, end_load, 0)

    def phase_a(slot, carry):
        t = coords[0, 0, 0, 0, slot]
        a = jnp.concatenate([ublk[0, t], ublk[1, t]], axis=0)
        b = item_rows(slot)
        g = gblk[coords[0, 0, 2, 0, slot]].astype(BF16)
        scale = lax.shift_left(jnp.int32(1), exps[0, 0, 0, slot] + 30).astype(F32) * (
            2.0**-30
        )
        term = jnp.zeros((TI, RANK), F32)
        for k in range(0, DEPTH, step):
            ag = (a[None] * g[k : k + step][:, None, :]).reshape(step * TU, RANK)
            model = lax.dot_general(
                ag, b, (((1,), (1,)), ((), ())), preferred_element_type=F32
            )
            w = wbuf[slot, k : k + step].reshape(step * TU, TI).astype(F32)
            v = vbuf[slot, k : k + step].reshape(step * TU, TI).astype(F32)
            err = (w * (model - v * scale)).astype(BF16)
            for n in range(step):
                errs[slot, 0, k + n] = err[n * TU : n * TU + 64]
                errs[slot, 1, k + n] = err[n * TU + 64 : n * TU + TU]
            term = term + lax.dot_general(
                err, ag, (((0,), (0,)), ((), ())), preferred_element_type=F32
            )
        iterms[slot + 1] = term + iterms[prev[1, slot]]
        return carry

    def phase_b(order, slot, carry):
        half = core if order else 1 - core
        a = ublk[half, coords[0, 0, 0, 0, slot]].astype(F32)
        b = item_rows(slot)
        g = gblk[coords[0, 0, 2, 0, slot]]
        total = jnp.zeros((64, RANK), F32)
        rows = []
        for k in range(DEPTH):
            proj = jnp.dot(errs[slot, half, k], b, preferred_element_type=F32)
            total = total + proj * g[k : k + 1]
            rows.append(jnp.sum(proj * a, axis=0, keepdims=True))
        uterms[order, slot + 1] = total + uterms[order, prev[0, slot]]
        cterms[order, slot + 1] = (
            jnp.concatenate(rows, axis=0) + cterms[order, prev[2, slot]]
        )
        return carry

    lax.fori_loop(0, SLOTS, phase_a, 0, unroll=4)

    for t in range(IT):
        rows = iterms[last[1, t]]
        isum[0, 2 * t] = rows[:32]
        isum[1, 2 * t] = rows[32:64]
        isum[0, 2 * t + 1] = rows[64:96]
        isum[1, 2 * t + 1] = rows[96:]
    item_mate = copy_to(isum.at[1 - core], imate, rsend.at[1], rrecv.at[1], mate)
    item_mate.start()

    lax.fori_loop(0, SLOTS, functools.partial(phase_b, 0), 0, unroll=4)

    for t in range(UT):
        usum[t] = uterms[0, last[0, t]]
    user_mate = copy_to(usum, umate, rsend.at[0], rrecv.at[0], mate)
    user_mate.start()

    item_mate.wait()

    def pack_item(j, carry):
        rows = imate[j] + isum[core, j]
        imate[j] = rows
        isend[j, :32], isend[j, 32:33] = pack(rows)
        return carry

    lax.fori_loop(0, 16, pack_item, 0, unroll=4)

    def scatter_item(d, carry):
        j = (ij + d) % 16
        copy_to(
            isend.at[j, pl.ds(0, 33)],
            irecv.at[ij, pl.ds(0, 33)],
            rsend.at[3],
            rrecv.at[3],
            item_peer(d),
        ).start()
        return carry

    lax.fori_loop(1, 16, scatter_item, 0)

    lax.fori_loop(0, SLOTS, functools.partial(phase_b, 1), 0, unroll=4)

    user_mate.wait()

    def pack_user(j, carry):
        rows = umate[j] + uterms[1, last[0, j]]
        umate[j] = rows
        usend[j, :64], usend[j, 64:65] = pack(rows)
        return carry

    lax.fori_loop(0, 8, pack_user, 0, unroll=4)

    def scatter_user(d, carry):
        j = (uj + d) % 8
        copy_to(
            usend.at[j, pl.ds(0, 65)],
            urecv.at[uj, pl.ds(0, 65)],
            rsend.at[2],
            rrecv.at[2],
            user_peer(d),
        ).start()
        return carry

    lax.fori_loop(1, 8, scatter_user, 0)

    def pack_ctx(t, carry):
        rows = cterms[0, last[2, t]] + cterms[1, last[2, t]]
        csum[2 * t] = rows[:8]
        csum[2 * t + 1] = rows[8:]
        csend[2 * t, :8], csend[2 * t, 8:9] = pack(rows[:8])
        csend[2 * t + 1, :8], csend[2 * t + 1, 8:9] = pack(rows[8:])
        return carry

    lax.fori_loop(0, CT, pack_ctx, 0, unroll=4)

    def scatter_ctx(d, carry):
        j = (cj + d) % 32
        copy_to(
            csend.at[j, pl.ds(0, 9)],
            crecv.at[cj, pl.ds(0, 9)],
            rsend.at[4],
            rrecv.at[4],
            ctx_peer(d),
        ).start()
        return carry

    lax.fori_loop(1, 32, scatter_ctx, 0)

    wait_bytes(irecv.at[pl.ds(0, 15), pl.ds(0, 33)], rrecv.at[3])
    total = imate[ij]
    for d in range(1, 16):
        total = total + unpack(irecv, (ij + d) % 16, 32)
    ig_out[...] = total
    wait_bytes(urecv.at[pl.ds(0, 7), pl.ds(0, 65)], rrecv.at[2])
    total = umate[uj]
    for d in range(1, 8):
        total = total + unpack(urecv, (uj + d) % 8, 64)
    ug_out[...] = total
    wait_bytes(crecv.at[pl.ds(0, 31), pl.ds(0, 9)], rrecv.at[4])
    total = csum[cj]
    for d in range(1, 32):
        total = total + unpack(crecv, (cj + d) % 32, 8)
    cg_out[...] = total
    wait_bytes(urecv.at[pl.ds(0, 7), pl.ds(0, 65)], rsend.at[2])
    wait_bytes(irecv.at[pl.ds(0, 15), pl.ds(0, 33)], rsend.at[3])
    wait_bytes(crecv.at[pl.ds(0, 31), pl.ds(0, 9)], rsend.at[4])


def copy_out(ug, ig, cg, ug_out, ig_out, cg_out):
    ug_out[...] = ug[...]
    ig_out[...] = ig[...]
    cg_out[...] = cg[...]


def local(
    values,
    weights,
    exps,
    coords,
    counts,
    uf,
    itf,
    cf,
):
    hbm = pl.BlockSpec(memory_space=pltpu.HBM)
    smem = pl.BlockSpec(memory_space=pltpu.SMEM)
    vmem = pl.BlockSpec(memory_space=pltpu.VMEM)
    dma = pltpu.SemaphoreType.DMA
    grads = pl.pallas_call(
        kernel,
        in_specs=[hbm, hbm, smem, smem, smem, vmem, vmem, vmem],
        out_specs=[vmem, vmem, vmem],
        out_shape=[
            jax.ShapeDtypeStruct(uf.shape, F32),
            jax.ShapeDtypeStruct(itf.shape, F32),
            jax.ShapeDtypeStruct(cf.shape, F32),
        ],
        scratch_shapes=[
            pltpu.VMEM((SLOTS, DEPTH, TU, TI), BF16),
            pltpu.VMEM((SLOTS, DEPTH, TU, TI), BF16),
            pltpu.VMEM((2, 8, 64, RANK), BF16),
            pltpu.VMEM((2, 16, 32, RANK), BF16),
            pltpu.VMEM((16, 128), BF16),
            pltpu.VMEM((32, 16, 128), BF16),
            pltpu.VMEM((CT, DEPTH, RANK), F32),
            pltpu.VMEM((SLOTS, 2, DEPTH, 64, TI), BF16),
            pltpu.VMEM((SLOTS + 1, TI, RANK), F32),
            pltpu.VMEM((2, SLOTS + 1, 64, RANK), F32),
            pltpu.VMEM((2, SLOTS + 1, DEPTH, RANK), F32),
            pltpu.SMEM((3, SLOTS), jnp.int32),
            pltpu.SMEM((3, CT), jnp.int32),
            pltpu.VMEM((8, 64, RANK), F32),
            pltpu.VMEM((2, 16, 32, RANK), F32),
            pltpu.VMEM((32, 8, RANK), F32),
            pltpu.VMEM((8, 64, RANK), F32),
            pltpu.VMEM((16, 32, RANK), F32),
            pltpu.VMEM((8, 72, 128), jnp.int32),
            pltpu.VMEM((16, 40, 128), jnp.int32),
            pltpu.VMEM((32, 16, 128), jnp.int32),
            pltpu.VMEM((8, 72, 128), jnp.int32),
            pltpu.VMEM((16, 40, 128), jnp.int32),
            pltpu.VMEM((32, 16, 128), jnp.int32),
            dma((2, SLOTS)),
            dma((5,)),
            dma((5,)),
            dma((5,)),
            dma((5,)),
        ],
        compiler_params=pltpu.CompilerParams(
            collective_id=0,
            has_side_effects=True,
            vmem_limit_bytes=56 * 2**20,
        ),
        name="cp_gradient",
    )(values, weights, exps, jnp.transpose(coords, (0, 1, 4, 2, 3)), counts, uf, itf, cf)
    return pl.pallas_call(
        copy_out,
        in_specs=[vmem] * 3,
        out_specs=[vmem] * 3,
        out_shape=[jax.ShapeDtypeStruct(g.shape, F32) for g in grads],
        name="copy_out",
    )(*grads)


def solution(mesh):
    placed = (
        P("user", "item", "ctx", None, None, None, None),
        P("user", "item", "ctx", None, None, None, None),
        P("user", "item", "ctx", None),
        P("user", "item", "ctx", None, None),
        P("user", "item", "ctx"),
        P(("user", "item", "ctx"), None),
        P(("item", "user", "ctx"), None),
        P(("ctx", "user", "item"), None),
    )
    return jax.shard_map(
        local,
        mesh=mesh,
        in_specs=placed,
        out_specs=(
            P(("user", "item", "ctx"), None),
            P(("item", "user", "ctx"), None),
            P(("ctx", "user", "item"), None),
        ),
        check_vma=False,
    )
```

```python
import functools

import jax
import jax.numpy as jnp
from jax import lax
from jax.experimental import pallas as pl
from jax.experimental.pallas import tpu as pltpu
from jax.sharding import PartitionSpec as P

MESH = pl.DeviceIdType.MESH
F32 = jnp.float32
BF16 = jnp.bfloat16
SLOTS, DEPTH, TU, TI, RANK = 16, 16, 128, 128, 256
UT, IT, CT = 8, 8, 16
NU, NI, NC = 8, 4, 4


def copy_to(src, dst, send, recv, device):
    return pltpu.make_async_remote_copy(
        src_ref=src,
        dst_ref=dst,
        send_sem=send,
        recv_sem=recv,
        device_id=device,
        device_id_type=MESH,
    )


def wait_bytes(ref, sem):
    pltpu.make_async_copy(ref, ref, sem).wait()


def pack(rows):
    left, right = rows[:, :128], rows[:, 128:]
    peak = jnp.max(jnp.maximum(jnp.abs(left), jnp.abs(right)), axis=0, keepdims=True)
    power = jnp.floor(jnp.log2(jnp.maximum(peak, 2.0**-90))) + 1.0
    scale = jnp.exp2(-power) * 32000.0
    high = jnp.round(left * scale).astype(jnp.int32)
    low = jnp.round(right * scale).astype(jnp.int32)
    codes = lax.shift_left(high, 16) | (low & 0xFFFF)
    return codes, power.astype(jnp.int32)


def unpack(codes, power):
    step = jnp.exp2(power.astype(F32)) * (1.0 / 32000.0)
    high = lax.shift_right_arithmetic(codes, 16).astype(F32)
    low = lax.shift_right_arithmetic(lax.shift_left(codes, 16), 16).astype(F32)
    return jnp.concatenate([high * step, low * step], axis=1)


def kernel(
    values,
    weights,
    exps,
    coords,
    counts,
    uf,
    itf,
    cf,
    ug_out,
    ig_out,
    cg_out,
    vbuf,
    wbuf,
    ublk,
    iblk,
    cstage,
    cblk,
    gblk,
    errs,
    iterms,
    uterms,
    cterms,
    prev,
    last,
    usum,
    isum,
    csum,
    umate,
    imate,
    usend,
    isend,
    csend,
    urecv,
    irecv,
    crecv,
    load_sem,
    gsend,
    grecv,
    rsend,
    rrecv,
):
    u = lax.axis_index("user")
    i = lax.axis_index("item")
    c = lax.axis_index("ctx")
    ylo = c // 2
    core = c % 2
    mate = (u, i, ylo * 2 + 1 - core)
    uj = i * 2 + ylo
    ij = u * 2 + ylo
    cj = u * 4 + i

    def load(slot):
        return (
            pltpu.make_async_copy(
                values.at[0, 0, 0, slot], vbuf.at[slot], load_sem.at[0, slot]
            ),
            pltpu.make_async_copy(
                weights.at[0, 0, 0, slot], wbuf.at[slot], load_sem.at[1, slot]
            ),
        )

    def start_load(slot, carry):
        for copy in load(slot):
            copy.start()
        return carry

    def user_peer(d):
        j = (uj + d) % 8
        return (u, j // 2, (j % 2) * 2 + core)

    def item_peer(d):
        j = (ij + d) % 16
        return (j // 2, i, (j % 2) * 2 + core)

    def ctx_peer(d):
        j = (cj + d) % 32
        return (j // 4, j % 4, c)

    barrier = pltpu.get_barrier_semaphore()

    def greet(peer, n):
        def one(d, carry):
            pl.semaphore_signal(barrier, inc=1, device_id=peer(d), device_id_type=MESH)
            return carry

        lax.fori_loop(1, n, one, 0)

    greet(user_peer, 8)
    greet(item_peer, 16)
    greet(ctx_peer, 32)
    pl.semaphore_signal(barrier, inc=1, device_id=mate, device_id_type=MESH)

    pl.semaphore_wait(barrier, 7 + 15 + 31 + 1)

    def gather_user(d, carry):
        copy_to(uf, ublk.at[core, uj], gsend.at[0], grecv.at[0], user_peer(d)).start()
        return carry

    def gather_item(d, carry):
        copy_to(itf, iblk.at[core, ij], gsend.at[1], grecv.at[1], item_peer(d)).start()
        return carry

    def gather_ctx(d, carry):
        copy_to(cstage, cblk.at[cj], gsend.at[2], grecv.at[2], ctx_peer(d)).start()
        return carry

    lax.fori_loop(1, 16, gather_item, 0)
    lax.fori_loop(1, 8, gather_user, 0)

    ublk[core, uj] = uf[...]
    iblk[core, ij] = itf[...]
    own = cf[...].astype(F32)
    cstage[...] = jnp.concatenate([own[:, :128], own[:, 128:]], axis=0).astype(BF16)
    cblk[cj] = cstage[...]

    lax.fori_loop(1, 32, gather_ctx, 0)
    lax.fori_loop(0, SLOTS, start_load, 0)

    count = counts[0, 0, 0]
    tile = [[coords[0, 0, m, 0, s] for s in range(SLOTS)] for m in range(3)]
    for m in range(3):
        for s in range(SLOTS):
            entry = jnp.int32(0)
            for t in range(s):
                entry = jnp.where(tile[m][t] == tile[m][s], t + 1, entry)
            prev[m, s] = entry
        for n in range((UT, IT, CT)[m]):
            entry = jnp.int32(0)
            for s in range(SLOTS):
                hit = jnp.logical_and(tile[m][s] == n, s < count)
                entry = jnp.where(hit, s + 1, entry)
            last[m, n] = entry
    iterms[0] = jnp.zeros((TI, RANK), F32)
    for order in range(2):
        uterms[order, 0] = jnp.zeros((64, RANK), F32)
        cterms[order, 0] = jnp.zeros((DEPTH, RANK), F32)

    wait_bytes(iblk.at[0, pl.ds(0, 15)], grecv.at[1])
    item_forward = copy_to(
        iblk.at[core], iblk.at[core], gsend.at[3], grecv.at[3], mate
    )
    item_forward.start()
    wait_bytes(ublk.at[0, pl.ds(0, 7)], grecv.at[0])
    user_forward = copy_to(
        ublk.at[core], ublk.at[core], gsend.at[4], grecv.at[4], mate
    )
    user_forward.start()
    wait_bytes(cblk.at[pl.ds(0, 31)], grecv.at[2])

    def unpack_ctx(t, carry):
        rows = []
        for half in range(2):
            pair = cblk[2 * t + half].astype(F32)
            rows.append(jnp.concatenate([pair[:8], pair[8:]], axis=1))
        gblk[t] = jnp.concatenate(rows, axis=0)
        return carry

    lax.fori_loop(0, CT, unpack_ctx, 0)
    item_forward.wait()
    user_forward.wait()
    wait_bytes(ublk.at[0, pl.ds(0, 7)], gsend.at[0])
    wait_bytes(iblk.at[0, pl.ds(0, 15)], gsend.at[1])
    wait_bytes(cblk.at[pl.ds(0, 31)], gsend.at[2])

    def item_rows(slot):
        t = coords[0, 0, 1, 0, slot]
        return jnp.concatenate(
            [
                iblk[0, 2 * t],
                iblk[1, 2 * t],
                iblk[0, 2 * t + 1],
                iblk[1, 2 * t + 1],
            ],
            axis=0,
        )

    step = 4

    def end_load(slot, carry):
        for copy in load(slot):
            copy.wait()
        return carry

    lax.fori_loop(0, SLOTS, end_load, 0)

    def phase_a(slot, carry):
        t = coords[0, 0, 0, 0, slot]
        a = jnp.concatenate([ublk[0, t], ublk[1, t]], axis=0)
        b = item_rows(slot)
        g = gblk[coords[0, 0, 2, 0, slot]].astype(BF16)
        scale = lax.shift_left(jnp.int32(1), exps[0, 0, 0, slot] + 30).astype(F32) * (
            2.0**-30
        )
        for k in range(0, DEPTH, step):
            ag = (a[None] * g[k : k + step][:, None, :]).reshape(step * TU, RANK)
            model = lax.dot_general(
                ag, b, (((1,), (1,)), ((), ())), preferred_element_type=F32
            )
            w = wbuf[slot, k : k + step].reshape(step * TU, TI).astype(F32)
            v = vbuf[slot, k : k + step].reshape(step * TU, TI).astype(F32)
            err = (w * (model - v * scale)).astype(BF16)
            for n in range(step):
                errs[slot, 0, k + n] = err[n * TU : n * TU + 64]
                errs[slot, 1, k + n] = err[n * TU + 64 : n * TU + TU]
        return carry

    def phase_item(slot, carry):
        t = coords[0, 0, 0, 0, slot]
        a = jnp.concatenate([ublk[0, t], ublk[1, t]], axis=0)
        g = gblk[coords[0, 0, 2, 0, slot]].astype(BF16)
        term = jnp.zeros((TI, RANK), F32)
        for k in range(0, DEPTH, step):
            ag = (a[None] * g[k : k + step][:, None, :]).reshape(step * TU, RANK)
            err = jnp.concatenate(
                [errs[slot, half, k + n] for n in range(step) for half in range(2)],
                axis=0,
            )
            term = term + lax.dot_general(
                err, ag, (((0,), (0,)), ((), ())), preferred_element_type=F32
            )
        iterms[slot + 1] = term + iterms[prev[1, slot]]
        return carry

    def phase_b(order, slot, carry):
        half = core if order else 1 - core
        a = ublk[half, coords[0, 0, 0, 0, slot]].astype(F32)
        b = item_rows(slot)
        g = gblk[coords[0, 0, 2, 0, slot]]
        total = jnp.zeros((64, RANK), F32)
        rows = []
        for k in range(DEPTH):
            proj = jnp.dot(errs[slot, half, k], b, preferred_element_type=F32)
            total = total + proj * g[k : k + 1]
            rows.append(jnp.sum(proj * a, axis=0, keepdims=True))
        uterms[order, slot + 1] = total + uterms[order, prev[0, slot]]
        cterms[order, slot + 1] = (
            jnp.concatenate(rows, axis=0) + cterms[order, prev[2, slot]]
        )
        return carry

    lax.fori_loop(0, SLOTS, phase_a, 0, unroll=4)
    lax.fori_loop(0, SLOTS, phase_item, 0, unroll=4)

    for t in range(IT):
        rows = iterms[last[1, t]]
        isum[0, 2 * t] = rows[:32]
        isum[1, 2 * t] = rows[32:64]
        isum[0, 2 * t + 1] = rows[64:96]
        isum[1, 2 * t + 1] = rows[96:]
    item_mate = copy_to(isum.at[1 - core], imate, rsend.at[1], rrecv.at[1], mate)
    item_mate.start()

    early = SLOTS // 2
    lax.fori_loop(0, early, functools.partial(phase_b, 0), 0, unroll=4)

    item_mate.wait()

    def pack_item(j, carry):
        rows = imate[j] + isum[core, j]
        imate[j] = rows
        isend[j, :32], isend[j, 32:33] = pack(rows)
        return carry

    lax.fori_loop(0, 16, pack_item, 0, unroll=4)

    def scatter_item(d, carry):
        j = (ij + d) % 16
        copy_to(
            isend.at[j, pl.ds(0, 33)],
            irecv.at[ij, pl.ds(0, 33)],
            rsend.at[3],
            rrecv.at[3],
            item_peer(d),
        ).start()
        return carry

    lax.fori_loop(1, 16, scatter_item, 0)

    lax.fori_loop(early, SLOTS, functools.partial(phase_b, 0), 0, unroll=4)

    for t in range(UT):
        usum[t] = uterms[0, last[0, t]]
    user_mate = copy_to(usum, umate, rsend.at[0], rrecv.at[0], mate)
    user_mate.start()

    lax.fori_loop(0, SLOTS, functools.partial(phase_b, 1), 0, unroll=4)

    def pack_ctx(t, carry):
        rows = cterms[0, last[2, t]] + cterms[1, last[2, t]]
        csum[2 * t] = rows[:8]
        csum[2 * t + 1] = rows[8:]
        csend[2 * t, :8], csend[2 * t, 8:9] = pack(rows[:8])
        csend[2 * t + 1, :8], csend[2 * t + 1, 8:9] = pack(rows[8:])
        return carry

    lax.fori_loop(0, CT, pack_ctx, 0, unroll=4)

    def scatter_ctx(d, carry):
        j = (cj + d) % 32
        copy_to(
            csend.at[j, pl.ds(0, 9)],
            crecv.at[cj, pl.ds(0, 9)],
            rsend.at[4],
            rrecv.at[4],
            ctx_peer(d),
        ).start()
        return carry

    lax.fori_loop(1, 32, scatter_ctx, 0)

    user_mate.wait()

    def pack_user(j, carry):
        rows = umate[j] + uterms[1, last[0, j]]
        umate[j] = rows
        usend[j, :64], usend[j, 64:65] = pack(rows)
        return carry

    lax.fori_loop(0, 8, pack_user, 0, unroll=4)

    def scatter_user(d, carry):
        j = (uj + d) % 8
        copy_to(
            usend.at[j, pl.ds(0, 65)],
            urecv.at[uj, pl.ds(0, 65)],
            rsend.at[2],
            rrecv.at[2],
            user_peer(d),
        ).start()
        return carry

    lax.fori_loop(1, 8, scatter_user, 0)

    wait_bytes(irecv.at[pl.ds(0, 15), pl.ds(0, 33)], rrecv.at[3])
    total = imate[ij]
    for d in range(1, 16):
        j = (ij + d) % 16
        total = total + unpack(irecv[j, :32], irecv[j, 32:33])
    ig_out[...] = total
    wait_bytes(urecv.at[pl.ds(0, 7), pl.ds(0, 65)], rrecv.at[2])
    total = umate[uj]
    for d in range(1, 8):
        j = (uj + d) % 8
        total = total + unpack(urecv[j, :64], urecv[j, 64:65])
    ug_out[...] = total
    wait_bytes(crecv.at[pl.ds(0, 31), pl.ds(0, 9)], rrecv.at[4])
    total = csum[cj]
    for d in range(1, 32):
        j = (cj + d) % 32
        total = total + unpack(crecv[j, :8], crecv[j, 8:9])
    cg_out[...] = total
    wait_bytes(urecv.at[pl.ds(0, 7), pl.ds(0, 65)], rsend.at[2])
    wait_bytes(irecv.at[pl.ds(0, 15), pl.ds(0, 33)], rsend.at[3])
    wait_bytes(crecv.at[pl.ds(0, 31), pl.ds(0, 9)], rsend.at[4])


def copy_out(ug, ig, cg, ug_out, ig_out, cg_out):
    ug_out[...] = ug[...]
    ig_out[...] = ig[...]
    cg_out[...] = cg[...]


def local(
    values,
    weights,
    exps,
    coords,
    counts,
    uf,
    itf,
    cf,
):
    hbm = pl.BlockSpec(memory_space=pltpu.HBM)
    smem = pl.BlockSpec(memory_space=pltpu.SMEM)
    vmem = pl.BlockSpec(memory_space=pltpu.VMEM)
    dma = pltpu.SemaphoreType.DMA
    grads = pl.pallas_call(
        kernel,
        in_specs=[hbm, hbm, smem, smem, smem, vmem, vmem, vmem],
        out_specs=[vmem, vmem, vmem],
        out_shape=[
            jax.ShapeDtypeStruct(uf.shape, F32),
            jax.ShapeDtypeStruct(itf.shape, F32),
            jax.ShapeDtypeStruct(cf.shape, F32),
        ],
        scratch_shapes=[
            pltpu.VMEM((SLOTS, DEPTH, TU, TI), BF16),
            pltpu.VMEM((SLOTS, DEPTH, TU, TI), BF16),
            pltpu.VMEM((2, 8, 64, RANK), BF16),
            pltpu.VMEM((2, 16, 32, RANK), BF16),
            pltpu.VMEM((16, 128), BF16),
            pltpu.VMEM((32, 16, 128), BF16),
            pltpu.VMEM((CT, DEPTH, RANK), F32),
            pltpu.VMEM((SLOTS, 2, DEPTH, 64, TI), BF16),
            pltpu.VMEM((SLOTS + 1, TI, RANK), F32),
            pltpu.VMEM((2, SLOTS + 1, 64, RANK), F32),
            pltpu.VMEM((2, SLOTS + 1, DEPTH, RANK), F32),
            pltpu.SMEM((3, SLOTS), jnp.int32),
            pltpu.SMEM((3, CT), jnp.int32),
            pltpu.VMEM((8, 64, RANK), F32),
            pltpu.VMEM((2, 16, 32, RANK), F32),
            pltpu.VMEM((32, 8, RANK), F32),
            pltpu.VMEM((8, 64, RANK), F32),
            pltpu.VMEM((16, 32, RANK), F32),
            pltpu.VMEM((8, 72, 128), jnp.int32),
            pltpu.VMEM((16, 40, 128), jnp.int32),
            pltpu.VMEM((32, 16, 128), jnp.int32),
            pltpu.VMEM((8, 72, 128), jnp.int32),
            pltpu.VMEM((16, 40, 128), jnp.int32),
            pltpu.VMEM((32, 16, 128), jnp.int32),
            dma((2, SLOTS)),
            dma((5,)),
            dma((5,)),
            dma((5,)),
            dma((5,)),
        ],
        compiler_params=pltpu.CompilerParams(
            collective_id=0,
            has_side_effects=True,
            vmem_limit_bytes=56 * 2**20,
        ),
        name="cp_gradient",
    )(values, weights, exps, jnp.transpose(coords, (0, 1, 4, 2, 3)), counts, uf, itf, cf)
    return pl.pallas_call(
        copy_out,
        in_specs=[vmem] * 3,
        out_specs=[vmem] * 3,
        out_shape=[jax.ShapeDtypeStruct(g.shape, F32) for g in grads],
        name="copy_out",
    )(*grads)


def solution(mesh):
    placed = (
        P("user", "item", "ctx", None, None, None, None),
        P("user", "item", "ctx", None, None, None, None),
        P("user", "item", "ctx", None),
        P("user", "item", "ctx", None, None),
        P("user", "item", "ctx"),
        P(("user", "item", "ctx"), None),
        P(("item", "user", "ctx"), None),
        P(("ctx", "user", "item"), None),
    )
    return jax.shard_map(
        local,
        mesh=mesh,
        in_specs=placed,
        out_specs=(
            P(("user", "item", "ctx"), None),
            P(("item", "user", "ctx"), None),
            P(("ctx", "user", "item"), None),
        ),
        check_vma=False,
    )
```

```python
import functools

import jax
import jax.numpy as jnp
from jax import lax
from jax.experimental import pallas as pl
from jax.experimental.pallas import tpu as pltpu
from jax.sharding import PartitionSpec as P

MESH = pl.DeviceIdType.MESH
F32 = jnp.float32
BF16 = jnp.bfloat16
SLOTS, DEPTH, TU, TI, RANK = 16, 16, 128, 128, 256
UT, IT, CT = 8, 8, 16
NU, NI, NC = 8, 4, 4


def copy_to(src, dst, send, recv, device):
    return pltpu.make_async_remote_copy(
        src_ref=src,
        dst_ref=dst,
        send_sem=send,
        recv_sem=recv,
        device_id=device,
        device_id_type=MESH,
    )


def wait_bytes(ref, sem):
    pltpu.make_async_copy(ref, ref, sem).wait()


def pack(rows):
    left, right = rows[:, :128], rows[:, 128:]
    peak = jnp.max(jnp.maximum(jnp.abs(left), jnp.abs(right)), axis=0, keepdims=True)
    power = jnp.floor(jnp.log2(jnp.maximum(peak, 2.0**-90))) + 1.0
    scale = jnp.exp2(-power) * 32000.0
    high = jnp.round(left * scale).astype(jnp.int32)
    low = jnp.round(right * scale).astype(jnp.int32)
    codes = lax.shift_left(high, 16) | (low & 0xFFFF)
    return codes, power.astype(jnp.int32)


def unpack(codes, power):
    step = jnp.exp2(power.astype(F32)) * (1.0 / 32000.0)
    high = lax.shift_right_arithmetic(codes, 16).astype(F32)
    low = lax.shift_right_arithmetic(lax.shift_left(codes, 16), 16).astype(F32)
    return jnp.concatenate([high * step, low * step], axis=1)


def kernel(
    values,
    weights,
    exps,
    coords,
    counts,
    uf,
    itf,
    cf,
    ug_out,
    ig_out,
    cg_out,
    vbuf,
    wbuf,
    ublk,
    iblk,
    cstage,
    cblk,
    gblk,
    errs,
    iterms,
    uterms,
    cterms,
    prev,
    last,
    usum,
    isum,
    csum,
    umate,
    imate,
    usend,
    isend,
    csend,
    urecv,
    irecv,
    crecv,
    load_sem,
    gsend,
    grecv,
    rsend,
    rrecv,
):
    u = lax.axis_index("user")
    i = lax.axis_index("item")
    c = lax.axis_index("ctx")
    ylo = c // 2
    core = c % 2
    mate = (u, i, ylo * 2 + 1 - core)
    uj = i * 2 + ylo
    ij = u * 2 + ylo
    cj = u * 4 + i

    def load(slot):
        return (
            pltpu.make_async_copy(
                values.at[0, 0, 0, slot], vbuf.at[slot], load_sem.at[0, slot]
            ),
            pltpu.make_async_copy(
                weights.at[0, 0, 0, slot], wbuf.at[slot], load_sem.at[1, slot]
            ),
        )

    def start_load(slot, carry):
        for copy in load(slot):
            copy.start()
        return carry

    def user_peer(d):
        j = (uj + d) % 8
        return (u, j // 2, (j % 2) * 2 + core)

    def item_peer(d):
        j = (ij + d) % 16
        return (j // 2, i, (j % 2) * 2 + core)

    def ctx_peer(d):
        j = (cj + d) % 32
        return (j // 4, j % 4, c)

    barrier = pltpu.get_barrier_semaphore()

    def greet(peer, n):
        def one(d, carry):
            pl.semaphore_signal(barrier, inc=1, device_id=peer(d), device_id_type=MESH)
            return carry

        lax.fori_loop(1, n, one, 0)

    greet(user_peer, 8)
    greet(item_peer, 16)
    greet(ctx_peer, 32)
    pl.semaphore_signal(barrier, inc=1, device_id=mate, device_id_type=MESH)

    pl.semaphore_wait(barrier, 7 + 15 + 31 + 1)

    def gather_user(d, carry):
        copy_to(uf, ublk.at[core, uj], gsend.at[0], grecv.at[0], user_peer(d)).start()
        return carry

    def gather_item(d, carry):
        copy_to(itf, iblk.at[core, ij], gsend.at[1], grecv.at[1], item_peer(d)).start()
        return carry

    def gather_ctx(d, carry):
        copy_to(cstage, cblk.at[cj], gsend.at[2], grecv.at[2], ctx_peer(d)).start()
        return carry

    lax.fori_loop(1, 16, gather_item, 0)
    lax.fori_loop(1, 8, gather_user, 0)

    ublk[core, uj] = uf[...]
    iblk[core, ij] = itf[...]
    own = cf[...].astype(F32)
    cstage[...] = jnp.concatenate([own[:, :128], own[:, 128:]], axis=0).astype(BF16)
    cblk[cj] = cstage[...]

    lax.fori_loop(1, 32, gather_ctx, 0)
    lax.fori_loop(0, SLOTS, start_load, 0)

    count = counts[0, 0, 0]
    tile = [[coords[0, 0, m, 0, s] for s in range(SLOTS)] for m in range(3)]
    for m in range(3):
        for s in range(SLOTS):
            entry = jnp.int32(0)
            for t in range(s):
                entry = jnp.where(tile[m][t] == tile[m][s], t + 1, entry)
            prev[m, s] = entry
        for n in range((UT, IT, CT)[m]):
            entry = jnp.int32(0)
            for s in range(SLOTS):
                hit = jnp.logical_and(tile[m][s] == n, s < count)
                entry = jnp.where(hit, s + 1, entry)
            last[m, n] = entry
    iterms[0] = jnp.zeros((TI, RANK), F32)
    for order in range(2):
        uterms[order, 0] = jnp.zeros((64, RANK), F32)
        cterms[order, 0] = jnp.zeros((DEPTH, RANK), F32)

    wait_bytes(iblk.at[0, pl.ds(0, 15)], grecv.at[1])
    item_forward = copy_to(
        iblk.at[core], iblk.at[core], gsend.at[3], grecv.at[3], mate
    )
    item_forward.start()
    wait_bytes(ublk.at[0, pl.ds(0, 7)], grecv.at[0])
    user_forward = copy_to(
        ublk.at[core], ublk.at[core], gsend.at[4], grecv.at[4], mate
    )
    user_forward.start()
    wait_bytes(cblk.at[pl.ds(0, 31)], grecv.at[2])

    def unpack_ctx(t, carry):
        rows = []
        for half in range(2):
            pair = cblk[2 * t + half].astype(F32)
            rows.append(jnp.concatenate([pair[:8], pair[8:]], axis=1))
        gblk[t] = jnp.concatenate(rows, axis=0)
        return carry

    lax.fori_loop(0, CT, unpack_ctx, 0)
    item_forward.wait()
    user_forward.wait()
    wait_bytes(ublk.at[0, pl.ds(0, 7)], gsend.at[0])
    wait_bytes(iblk.at[0, pl.ds(0, 15)], gsend.at[1])
    wait_bytes(cblk.at[pl.ds(0, 31)], gsend.at[2])

    def item_rows(slot):
        t = coords[0, 0, 1, 0, slot]
        return jnp.concatenate(
            [
                iblk[0, 2 * t],
                iblk[1, 2 * t],
                iblk[0, 2 * t + 1],
                iblk[1, 2 * t + 1],
            ],
            axis=0,
        )

    step = 4

    def end_load(slot, carry):
        for copy in load(slot):
            copy.wait()
        return carry

    lax.fori_loop(0, SLOTS, end_load, 0)

    def phase_a(slot, carry):
        t = coords[0, 0, 0, 0, slot]
        a = jnp.concatenate([ublk[0, t], ublk[1, t]], axis=0)
        b = item_rows(slot)
        g = gblk[coords[0, 0, 2, 0, slot]].astype(BF16)
        scale = lax.shift_left(jnp.int32(1), exps[0, 0, 0, slot] + 30).astype(F32) * (
            2.0**-30
        )
        for k in range(0, DEPTH, step):
            ag = (a[None] * g[k : k + step][:, None, :]).reshape(step * TU, RANK)
            model = lax.dot_general(
                ag, b, (((1,), (1,)), ((), ())), preferred_element_type=F32
            )
            w = wbuf[slot, k : k + step].reshape(step * TU, TI).astype(F32)
            v = vbuf[slot, k : k + step].reshape(step * TU, TI).astype(F32)
            err = (w * (model - v * scale)).astype(BF16)
            for n in range(step):
                errs[slot, 0, k + n] = err[n * TU : n * TU + 64]
                errs[slot, 1, k + n] = err[n * TU + 64 : n * TU + TU]
        return carry

    def phase_item(slot, carry):
        t = coords[0, 0, 0, 0, slot]
        a = jnp.concatenate([ublk[0, t], ublk[1, t]], axis=0)
        g = gblk[coords[0, 0, 2, 0, slot]].astype(BF16)
        term = jnp.zeros((TI, RANK), F32)
        for k in range(0, DEPTH, step):
            ag = (a[None] * g[k : k + step][:, None, :]).reshape(step * TU, RANK)
            err = jnp.concatenate(
                [errs[slot, half, k + n] for n in range(step) for half in range(2)],
                axis=0,
            )
            term = term + lax.dot_general(
                err, ag, (((0,), (0,)), ((), ())), preferred_element_type=F32
            )
        iterms[slot + 1] = term + iterms[prev[1, slot]]
        return carry

    def phase_b(order, slot, carry):
        half = core if order else 1 - core
        a = ublk[half, coords[0, 0, 0, 0, slot]].astype(F32)
        b = item_rows(slot)
        g = gblk[coords[0, 0, 2, 0, slot]]
        total = jnp.zeros((64, RANK), F32)
        rows = []
        for k in range(DEPTH):
            proj = jnp.dot(errs[slot, half, k], b, preferred_element_type=F32)
            total = total + proj * g[k : k + 1]
            rows.append(jnp.sum(proj * a, axis=0, keepdims=True))
        uterms[order, slot + 1] = total + uterms[order, prev[0, slot]]
        cterms[order, slot + 1] = (
            jnp.concatenate(rows, axis=0) + cterms[order, prev[2, slot]]
        )
        return carry

    lax.fori_loop(0, SLOTS, phase_a, 0, unroll=8)
    lax.fori_loop(0, SLOTS, phase_item, 0, unroll=4)

    for t in range(IT):
        rows = iterms[last[1, t]]
        isum[0, 2 * t] = rows[:32]
        isum[1, 2 * t] = rows[32:64]
        isum[0, 2 * t + 1] = rows[64:96]
        isum[1, 2 * t + 1] = rows[96:]
    item_mate = copy_to(isum.at[1 - core], imate, rsend.at[1], rrecv.at[1], mate)
    item_mate.start()

    early = SLOTS // 2
    lax.fori_loop(0, early, functools.partial(phase_b, 0), 0, unroll=4)

    item_mate.wait()

    def pack_item(j, carry):
        rows = imate[j] + isum[core, j]
        imate[j] = rows
        isend[j, :32], isend[j, 32:33] = pack(rows)
        return carry

    lax.fori_loop(0, 16, pack_item, 0, unroll=4)

    def scatter_item(d, carry):
        j = (ij + d) % 16
        copy_to(
            isend.at[j, pl.ds(0, 33)],
            irecv.at[ij, pl.ds(0, 33)],
            rsend.at[3],
            rrecv.at[3],
            item_peer(d),
        ).start()
        return carry

    lax.fori_loop(1, 16, scatter_item, 0)

    lax.fori_loop(early, SLOTS, functools.partial(phase_b, 0), 0, unroll=4)

    for t in range(UT):
        usum[t] = uterms[0, last[0, t]]
    user_mate = copy_to(usum, umate, rsend.at[0], rrecv.at[0], mate)
    user_mate.start()

    lax.fori_loop(0, SLOTS, functools.partial(phase_b, 1), 0, unroll=4)

    def pack_ctx(t, carry):
        rows = cterms[0, last[2, t]] + cterms[1, last[2, t]]
        csum[2 * t] = rows[:8]
        csum[2 * t + 1] = rows[8:]
        csend[2 * t, :8], csend[2 * t, 8:9] = pack(rows[:8])
        csend[2 * t + 1, :8], csend[2 * t + 1, 8:9] = pack(rows[8:])
        return carry

    lax.fori_loop(0, CT, pack_ctx, 0, unroll=4)

    def scatter_ctx(d, carry):
        j = (cj + d) % 32
        copy_to(
            csend.at[j, pl.ds(0, 9)],
            crecv.at[cj, pl.ds(0, 9)],
            rsend.at[4],
            rrecv.at[4],
            ctx_peer(d),
        ).start()
        return carry

    lax.fori_loop(1, 32, scatter_ctx, 0)

    user_mate.wait()

    def pack_user(j, carry):
        rows = umate[j] + uterms[1, last[0, j]]
        umate[j] = rows
        usend[j, :64], usend[j, 64:65] = pack(rows)
        return carry

    lax.fori_loop(0, 8, pack_user, 0, unroll=4)

    def scatter_user(d, carry):
        j = (uj + d) % 8
        copy_to(
            usend.at[j, pl.ds(0, 65)],
            urecv.at[uj, pl.ds(0, 65)],
            rsend.at[2],
            rrecv.at[2],
            user_peer(d),
        ).start()
        return carry

    lax.fori_loop(1, 8, scatter_user, 0)

    wait_bytes(irecv.at[pl.ds(0, 15), pl.ds(0, 33)], rrecv.at[3])
    total = imate[ij]
    for d in range(1, 16):
        j = (ij + d) % 16
        total = total + unpack(irecv[j, :32], irecv[j, 32:33])
    ig_out[...] = total
    wait_bytes(urecv.at[pl.ds(0, 7), pl.ds(0, 65)], rrecv.at[2])
    total = umate[uj]
    for d in range(1, 8):
        j = (uj + d) % 8
        total = total + unpack(urecv[j, :64], urecv[j, 64:65])
    ug_out[...] = total
    wait_bytes(crecv.at[pl.ds(0, 31), pl.ds(0, 9)], rrecv.at[4])
    total = csum[cj]
    for d in range(1, 32):
        j = (cj + d) % 32
        total = total + unpack(crecv[j, :8], crecv[j, 8:9])
    cg_out[...] = total
    wait_bytes(urecv.at[pl.ds(0, 7), pl.ds(0, 65)], rsend.at[2])
    wait_bytes(irecv.at[pl.ds(0, 15), pl.ds(0, 33)], rsend.at[3])
    wait_bytes(crecv.at[pl.ds(0, 31), pl.ds(0, 9)], rsend.at[4])


def copy_out(ug, ig, cg, ug_out, ig_out, cg_out):
    ug_out[...] = ug[...]
    ig_out[...] = ig[...]
    cg_out[...] = cg[...]


def local(
    values,
    weights,
    exps,
    coords,
    counts,
    uf,
    itf,
    cf,
):
    hbm = pl.BlockSpec(memory_space=pltpu.HBM)
    smem = pl.BlockSpec(memory_space=pltpu.SMEM)
    vmem = pl.BlockSpec(memory_space=pltpu.VMEM)
    dma = pltpu.SemaphoreType.DMA
    grads = pl.pallas_call(
        kernel,
        in_specs=[hbm, hbm, smem, smem, smem, vmem, vmem, vmem],
        out_specs=[vmem, vmem, vmem],
        out_shape=[
            jax.ShapeDtypeStruct(uf.shape, F32),
            jax.ShapeDtypeStruct(itf.shape, F32),
            jax.ShapeDtypeStruct(cf.shape, F32),
        ],
        scratch_shapes=[
            pltpu.VMEM((SLOTS, DEPTH, TU, TI), BF16),
            pltpu.VMEM((SLOTS, DEPTH, TU, TI), BF16),
            pltpu.VMEM((2, 8, 64, RANK), BF16),
            pltpu.VMEM((2, 16, 32, RANK), BF16),
            pltpu.VMEM((16, 128), BF16),
            pltpu.VMEM((32, 16, 128), BF16),
            pltpu.VMEM((CT, DEPTH, RANK), F32),
            pltpu.VMEM((SLOTS, 2, DEPTH, 64, TI), BF16),
            pltpu.VMEM((SLOTS + 1, TI, RANK), F32),
            pltpu.VMEM((2, SLOTS + 1, 64, RANK), F32),
            pltpu.VMEM((2, SLOTS + 1, DEPTH, RANK), F32),
            pltpu.SMEM((3, SLOTS), jnp.int32),
            pltpu.SMEM((3, CT), jnp.int32),
            pltpu.VMEM((8, 64, RANK), F32),
            pltpu.VMEM((2, 16, 32, RANK), F32),
            pltpu.VMEM((32, 8, RANK), F32),
            pltpu.VMEM((8, 64, RANK), F32),
            pltpu.VMEM((16, 32, RANK), F32),
            pltpu.VMEM((8, 72, 128), jnp.int32),
            pltpu.VMEM((16, 40, 128), jnp.int32),
            pltpu.VMEM((32, 16, 128), jnp.int32),
            pltpu.VMEM((8, 72, 128), jnp.int32),
            pltpu.VMEM((16, 40, 128), jnp.int32),
            pltpu.VMEM((32, 16, 128), jnp.int32),
            dma((2, SLOTS)),
            dma((5,)),
            dma((5,)),
            dma((5,)),
            dma((5,)),
        ],
        compiler_params=pltpu.CompilerParams(
            collective_id=0,
            has_side_effects=True,
            vmem_limit_bytes=56 * 2**20,
        ),
        name="cp_gradient",
    )(values, weights, exps, jnp.transpose(coords, (0, 1, 4, 2, 3)), counts, uf, itf, cf)
    return pl.pallas_call(
        copy_out,
        in_specs=[vmem] * 3,
        out_specs=[vmem] * 3,
        out_shape=[jax.ShapeDtypeStruct(g.shape, F32) for g in grads],
        name="copy_out",
    )(*grads)


def solution(mesh):
    placed = (
        P("user", "item", "ctx", None, None, None, None),
        P("user", "item", "ctx", None, None, None, None),
        P("user", "item", "ctx", None),
        P("user", "item", "ctx", None, None),
        P("user", "item", "ctx"),
        P(("user", "item", "ctx"), None),
        P(("item", "user", "ctx"), None),
        P(("ctx", "user", "item"), None),
    )
    return jax.shard_map(
        local,
        mesh=mesh,
        in_specs=placed,
        out_specs=(
            P(("user", "item", "ctx"), None),
            P(("item", "user", "ctx"), None),
            P(("ctx", "user", "item"), None),
        ),
        check_vma=False,
    )
```
